256 devices in a mesh: section: 2 (over y_lo), ep: 64 (over z, x, core), tp: 2 (over y_hi).
Axes of the slice: x: 4, y: 4 (y_hi: 2, y_lo: 2; y = y_hi * 2 + y_lo), z: 8, core: 2. Of those that a mesh axis runs over, the one named last changes fastest.
Arguments:
- prompt_latent: bfloat16 [8192, 576], P('ep'), may hold values from -6 to 6
- prompt_dest: int32 [8192, 1], P('ep'), may hold values from 0 to 63; in each aligned block of 128 rows (0 to 127, 128 to 255, ...) at most 4 rows name the same one
- prompt_slot: int32 [8192], P('ep'), may hold values from 0 to 7
- old_cache: bfloat16 [512, 128, 576], P('ep'), may hold values from -6 to 6
- cache_len: int32 [512], P('ep'), may hold values from 1 to 128, 32768 in all
- new_latent: bfloat16 [512, 4, 576], P('ep'), may hold values from -6 to 6
- dec_query: bfloat16 [512, 4, 128, 576], P('ep', None, ('section', 'tp')), may hold values from -48 to 48
- dec_states: bfloat16 [512, 4, 7168], P('ep', None, ('section', 'tp')), may hold values from -6 to 6
- moe_gain: float32 [7168], P(('section', 'tp')), may hold values from 0.1 to 1.9
- expert_ids: int32 [512, 4, 8], P('ep'), may hold values from 0 to 63, all different within a row; in each aligned block of 32 rows (0 to 31, 32 to 63, ..., all dimensions but the last counted through in order) at most 8 rows name the same one
- route_weight: int32 [512, 4, 8], P('ep'), may hold values from 1 to 1024
- w_gate: bfloat16 [64, 7168, 1024], P('ep', None, ('section', 'tp')), may hold values from -0.0625 to 0.0625
- w_up: bfloat16 [64, 7168, 1024], P('ep', None, ('section', 'tp')), may hold values from -0.0625 to 0.0625
- w_down: bfloat16 [64, 1024, 7168], P('ep', ('section', 'tp')), may hold values from -0.1875 to 0.1875
Outputs:
- attn_out: bfloat16 [512, 4, 128, 512], P('ep', None, ('section', 'tp'))
- moe_out: bfloat16 [512, 4, 7168], P('ep', None, ('section', 'tp'))
The draws below stay inside these ranges and needn't reach their ends.
Inputs may be any that keep to these rules, and one draw needn't show every extreme that they name: `prompt_dest`: the prompt tokens of one index of ep name one owner at most 4 times, and some owner exactly that often. `expert_ids`: each token names 8 different experts; the tokens of one index of ep name one expert at most 8 times, and some expert exactly that often.
All inputs are finite; a program needn't handle non-finite values. No bound on the sum of `cache_len` on one device may be relied on, other than what follows from the above.
Results may differ from the reference program's by a relative error of at most 0.015.
Values may be sent and summed in bfloat16 or wider, within the bound.
No kernel may reach another device: no remote copies, remote signals or barrier semaphores. Data moves between devices by JAX's collectives and lax.ppermute only.
A program may use at most 128 MiB of HBM per device.

```python
import math
import jax
import jax.numpy as jnp
import numpy as np
from jax import lax

D = 7168
HEADS = 128
LAT = 512
ROPE = 64
TOPK = 8
EH = 1024
STEPS = 4
SEQ_DEV = 8
OLD = 128
PTOK_DEV = 128
GROUP = 4
SEQS = 512
TOK_DEV = 32
PTOK = 8192
EXPERTS = 64
PEER_CAP = 4
E_CAP = 8
N_EP = 64


def common_cache(key):
    return jnp.clip(jax.random.normal(key, (SEQS, OLD, LAT + ROPE), jnp.float32), -6.0, 6.0)


def draw_old_cache(key, part):
    base = common_cache(key)
    return base.astype(jnp.bfloat16)


def draw_dec_query(key, part):
    key = jax.random.fold_in(key, 23)
    first = jax.random.fold_in(key, 0)
    drawn = jnp.clip(jax.random.normal(first, (SEQS, STEPS, HEADS, LAT + ROPE), jnp.float32), -6.0, 6.0)
    return drawn.astype(jnp.bfloat16)


def touch_ends(values, key, least, high):
    shape = values.shape
    spot = [jax.random.randint(jax.random.fold_in(key, axis), (), 0, shape[axis]) for axis in range(len(shape))]
    values = values.at[tuple(spot)].set(least)
    longest = shape.index(max(shape))
    spot[longest] = (spot[longest] + 1) % shape[longest]
    return values.at[tuple(spot)].set(high)


def block_scale(stream_key, dims, cuts, least, top_value):
    factor_of = 1.0
    for dim, blocks in cuts:
        heights = jax.random.uniform(jax.random.fold_in(jax.random.fold_in(stream_key, 6), dim), (blocks,), jnp.float32, least / len(cuts), top_value / len(cuts))
        factor_of = factor_of * jnp.repeat(jnp.exp(heights), dims[dim] // blocks).reshape((-1,) + (1,) * (len(dims) - 1 - dim))
    return factor_of


def split_up(count, total, most, skew):
    weights = [(1 << 20) // math.isqrt(standing ** skew) + 1 for standing in range(2, count + 1)]
    rest, holding = total - most - (count - 1), [1] * (count - 1)
    while rest > 0:
        free = [i for i in range(count - 1) if holding[i] < most]
        pool, remaining = sum([weights[i] for i in free]), rest
        for i in free:
            extra = min(most - holding[i], max(1, remaining * weights[i] // pool), rest)
            holding[i] = holding[i] + extra
            rest = rest - extra
    return np.array([most] + holding)


def uneven_parts(own_key, number_of, total, most, slope):
    if number_of == 2:
        one = jax.random.randint(own_key, (), max(1, total - most), min(most, total - 1) + 1)
        return jnp.stack([one, total - one])
    sizes = jnp.asarray(split_up(number_of, total, most, slope), jnp.int32)
    pairs = (number_of - 1) // 2
    giver, receiver = sizes[1:1 + 2 * pairs:2], sizes[2:2 + 2 * pairs:2]
    margin = jnp.minimum(giver - 1, most - receiver)
    shifted = jax.random.randint(jax.random.fold_in(own_key, 1), (pairs,), 0, 1 << 20) % (margin + 1)
    sizes = sizes.at[1:1 + 2 * pairs:2].set(giver - shifted).at[2:2 + 2 * pairs:2].set(receiver + shifted)
    return sizes[jax.random.permutation(jax.random.fold_in(own_key, 2), number_of)]


def routed_block(stream_key, own, number, rows, amount, top, limit, slope):
    order = jax.random.permutation(stream_key, amount)
    crowded, common = load_shares(amount, rows * top, limit, slope, True), load_shares(amount, rows * top, limit, slope, False)
    places = jnp.arange(amount)

    def named(tallies, rotation):
        used = int((tallies > 0).sum())
        fixed = max(1, used // 4)
        passed = fixed + (places - fixed + rotation * (used - fixed)) % max(1, amount - fixed)
        return jnp.zeros((amount,), jnp.int32).at[order[jnp.where(places < fixed, places, passed)]].set(jnp.asarray(tallies, jnp.int32))

    tallies = jnp.where(number % 4 == 0, named(crowded, number // 4), named(common, number - number // 4 - 1))
    mixed = jax.random.permutation(jax.random.fold_in(own, 3), amount)
    source_of, taker = mixed[0:amount // 2 * 2:2], mixed[1:amount // 2 * 2:2]
    slack = jnp.minimum(tallies[source_of] - 1, limit - tallies[taker]) // 2
    slack = jnp.where((source_of == order[0]) | (taker == order[0]) | (tallies[taker] == 0), 0, jnp.maximum(slack, 0))
    passed = jax.random.randint(jax.random.fold_in(own, 4), (amount // 2,), 0, 1 << 20) % (slack + 1)
    tallies = tallies.at[source_of].add(-passed).at[taker].add(passed)
    items = jnp.searchsorted(jnp.cumsum(tallies), jnp.arange(rows * top), side="right").astype(jnp.int32)
    listing = items.reshape(top, rows).T
    listing = listing[jax.random.permutation(jax.random.fold_in(own, 1), rows)]
    rotation = jax.random.randint(jax.random.fold_in(own, 2), (rows, 1), 0, top)
    return jnp.take_along_axis(listing, (jnp.arange(top)[None, :] + rotation) % top, axis=1)


def load_shares(count, total, bound, slope, full):
    portions = [(1 << 20) // math.isqrt(grade ** slope) + 1 for grade in range(1, count + 1)]
    largest = bound if full else min(bound, max(-(-total // count), total * portions[0] // sum(portions)))
    least = 1 if total - largest >= count - 1 else 0
    holding, surplus = [largest] + [least] * (count - 1), total - largest - least * (count - 1)
    while surplus > 0:
        free = [i for i in range(1, count) if holding[i] < largest] or [i for i in range(1, count) if holding[i] < bound]
        pool, budget = sum([portions[i] for i in free]), surplus
        for i in free:
            addition = min(bound - holding[i], max(1, budget * portions[i] // pool), surplus)
            holding[i] = holding[i] + addition
            surplus = surplus - addition
    return np.array(holding)


def centred(stream_key, shape, scale, bound, cuts=(), kind=jnp.bfloat16):
    values = jax.random.normal(stream_key, shape, jnp.float32) * scale
    if len(cuts) > 0:
        values = block_scale(stream_key, shape, cuts, -0.22, 0.18) * values
    return jnp.clip(values, min=-bound, max=bound).astype(kind)


def setup_inputs(seed: int = 0) -> dict:
    streams_of = jax.random.split(jax.random.key(seed), 15)
    prompt_latent = centred(streams_of[0], (PTOK, LAT + ROPE), 1.0, 6.0, ((0, 64),))
    prompt_dest_keys = jax.random.split(jax.random.fold_in(streams_of[1], 1), PTOK // PTOK_DEV)
    prompt_dest_turns = jax.random.permutation(jax.random.fold_in(streams_of[1], 3), PTOK // PTOK_DEV)
    prompt_dest = jax.vmap(lambda own, number: routed_block(jax.random.fold_in(streams_of[1], 2), own, number, PTOK_DEV, N_EP, 1, PEER_CAP, 2))(prompt_dest_keys, prompt_dest_turns).reshape((PTOK, 1))
    prompt_slot = touch_ends(jax.random.randint(streams_of[2], (PTOK,), 0, SEQ_DEV), jax.random.fold_in(streams_of[2], 1), 0, SEQ_DEV - 1).astype(jnp.int32)
    old_cache = draw_old_cache(jax.random.fold_in(streams_of[14], 71), 0)
    cache_len = uneven_parts(streams_of[4], SEQS, SEQS * OLD // 2, OLD, 1).astype(jnp.int32)
    new_latent = centred(streams_of[5], (SEQS, STEPS, LAT + ROPE), 1.0, 6.0, ((0, 64),))
    dec_query = draw_dec_query(jax.random.fold_in(streams_of[14], 71), 0)
    dec_states = centred(streams_of[7], (SEQS, STEPS, D), 1.0, 6.0, ((0, 64), (2, 4)))
    moe_gain = jnp.clip(1.0 + 0.18 * jax.random.normal(streams_of[8], (D,), jnp.float32), 0.1, 1.9)
    expert_ids_keys = jax.random.split(jax.random.fold_in(streams_of[9], 1), SEQS * STEPS // TOK_DEV)
    expert_ids_turns = jax.random.permutation(jax.random.fold_in(streams_of[9], 3), SEQS * STEPS // TOK_DEV)
    expert_ids = jax.vmap(lambda own, number: routed_block(jax.random.fold_in(streams_of[9], 2), own, number, TOK_DEV, EXPERTS, TOPK, E_CAP, 2))(expert_ids_keys, expert_ids_turns).reshape((SEQS, STEPS, TOPK))
    route_weight = touch_ends(jax.random.randint(streams_of[10], (SEQS, STEPS, TOPK), 1, 1025), jax.random.fold_in(streams_of[10], 1), 1, 1024).astype(jnp.int32)
    w_gate = centred(streams_of[11], (EXPERTS, D, EH), D ** -0.5, 0.0625, ((0, 64), (2, 4)))
    w_up = centred(streams_of[12], (EXPERTS, D, EH), D ** -0.5, 0.0625, ((0, 64), (2, 4)))
    w_down = centred(streams_of[13], (EXPERTS, EH, D), EH ** -0.5, 0.1875, ((0, 64), (1, 4)))
    return {"prompt_latent": prompt_latent, "prompt_dest": prompt_dest, "prompt_slot": prompt_slot, "old_cache": old_cache, "cache_len": cache_len, "new_latent": new_latent, "dec_query": dec_query, "dec_states": dec_states, "moe_gain": moe_gain, "expert_ids": expert_ids, "route_weight": route_weight, "w_gate": w_gate, "w_up": w_up, "w_down": w_down}


EPS = 1e-06
SCORE_SCALE = 192.0 ** (-0.5)

def ranks_of(labels, count):
    table = (labels[:, None] == jnp.arange(count, dtype=jnp.int32)[None, :]).astype(jnp.int32)
    before = jnp.cumsum(table, axis=0) - table
    return lax.optimization_barrier(jnp.sum(before * table, axis=1)).astype(jnp.int32)

def attend_one(pieces):
    query, old_rows, old_len, got_rows, got_live, new_rows = pieces
    keys = jnp.concatenate([old_rows, got_rows, new_rows], axis=0)
    flat_query = query.reshape(STEPS * HEADS, LAT + ROPE)
    scores = jnp.dot(flat_query, keys.T, preferred_element_type=jnp.float32) * SCORE_SCALE
    query_step = jnp.arange(STEPS * HEADS, dtype=jnp.int32) // HEADS
    old_live = jnp.broadcast_to((jnp.arange(OLD, dtype=jnp.int32) < old_len)[None, :], (STEPS * HEADS, OLD))
    mid_live = jnp.broadcast_to(got_live[None, :], (STEPS * HEADS, got_live.shape[0]))
    new_live = jnp.arange(STEPS, dtype=jnp.int32)[None, :] <= query_step[:, None]
    live = jnp.concatenate([old_live, mid_live, new_live], axis=1)
    masked = jnp.where(live, scores, -jnp.inf)
    top = lax.optimization_barrier(jnp.max(masked, axis=1, keepdims=True))
    weights = jnp.exp(masked - top)
    total = lax.optimization_barrier(jnp.sum(weights, axis=1, keepdims=True))
    probs = weights.astype(jnp.bfloat16)
    summed = jnp.dot(probs, keys[:, :LAT], preferred_element_type=jnp.float32)
    return (summed / total).astype(jnp.bfloat16).reshape(STEPS, HEADS, LAT)

def reference(prompt_latent, prompt_dest, prompt_slot, old_cache, cache_len, new_latent, dec_query, dec_states, moe_gain, expert_ids, route_weight, w_gate, w_up, w_down):
    seq_of = (prompt_dest[:, 0] * SEQ_DEV + prompt_slot).astype(jnp.int32)
    rank = ranks_of(seq_of, SEQS)
    per_seq = N_EP * PEER_CAP
    got = jnp.zeros((SEQS, per_seq, LAT + ROPE), jnp.bfloat16).at[seq_of, rank].set(prompt_latent)
    live = jnp.zeros((SEQS, per_seq), jnp.bool_).at[seq_of, rank].set(True)
    attn_out = lax.map(attend_one, (dec_query, old_cache, cache_len, got, live, new_latent))
    tokens = SEQS * STEPS
    states = dec_states.reshape(tokens, D).astype(jnp.float32)
    normed = (states * lax.rsqrt(lax.optimization_barrier(jnp.mean(states * states, axis=1, keepdims=True)) + EPS) * moe_gain).astype(jnp.bfloat16)
    pairs = tokens * TOPK
    expert_flat = expert_ids.reshape(pairs).astype(jnp.int32)
    expert_rank = ranks_of(expert_flat, EXPERTS)
    token_of = jnp.arange(pairs, dtype=jnp.int32) // TOPK
    index = jnp.zeros((EXPERTS, N_EP * E_CAP), jnp.int32).at[expert_flat, expert_rank].set(token_of)
    block = EH // GROUP

    def run_expert(pieces):
        rows_index, gate_w, up_w, down_w = pieces
        rows = normed[rows_index]
        gate = jnp.dot(rows, gate_w, preferred_element_type=jnp.float32)
        up = jnp.dot(rows, up_w, preferred_element_type=jnp.float32)
        hidden = (jax.nn.silu(gate) * up).astype(jnp.bfloat16)
        summed = jnp.zeros((rows.shape[0], D), jnp.float32)
        for group_idx in range(GROUP):
            part = jnp.dot(hidden[:, group_idx * block:(group_idx + 1) * block], down_w[group_idx * block:(group_idx + 1) * block], preferred_element_type=jnp.float32)
            rounded = lax.optimization_barrier(part.astype(jnp.bfloat16))
            summed = summed + rounded.astype(jnp.float32)
        return summed.astype(jnp.bfloat16)
    results = lax.map(run_expert, (index, w_gate, w_up, w_down))
    picked = results[expert_flat, expert_rank].astype(jnp.float32).reshape(tokens, TOPK, D)
    weight = route_weight.reshape(tokens, TOPK).astype(jnp.float32)
    share = weight / lax.optimization_barrier(jnp.sum(weight, axis=1, keepdims=True))
    mixed = lax.optimization_barrier(jnp.sum(picked * share[:, :, None], axis=1))
    return (attn_out, mixed.astype(jnp.bfloat16).reshape(SEQS, STEPS, D))
```

```python
import jax
import jax.numpy as jnp
from jax import lax
from jax.sharding import PartitionSpec as P

LAT = 512
EPS = 1e-06
SCORE_SCALE = 192.0 ** (-0.5)
NZ, NX, NC = 8, 4, 2
NY = 4
E_CAP = 8
PEER_CAP = 4
GROUP = ("section", "tp")


def z_perm(k):
    return [(i, (i // 8 + k) % NZ * 8 + i % 8) for i in range(64)]


def x_perm(dx, dc):
    return [(i, i // 8 * 8 + ((i // 2 + dx) % NX) * 2 + ((i % 2) ^ dc)) for i in range(64)]


def group_of_y(y):
    return (y % 2) * 2 + (y // 2) % 2


def y_perm(k):
    return [(group_of_y(y), group_of_y((y + k) % NY)) for y in range(NY)]


def over_z(v, k):
    return lax.ppermute(v, "ep", z_perm(k % NZ)) if k % NZ else v


def over_x(v, dx, dc):
    return lax.ppermute(v, "ep", x_perm(dx % NX, dc)) if dx % NX or dc else v


def over_y(v, k):
    return lax.ppermute(v, GROUP, y_perm(k % NY)) if k % NY else v


def dot(a, b):
    return jnp.dot(a, b, preferred_element_type=jnp.float32)


def strict_lower(n):
    i = jnp.arange(n, dtype=jnp.int32)
    return (i[:, None] > i[None, :]).astype(jnp.bfloat16)


def attention(prompt_latent, prompt_dest, prompt_slot, old_cache, cache_len, new_latent, dec_query):
    n_ep = lax.axis_size("ep")
    ptok_dev, width = prompt_latent.shape
    seq_dev, steps, heads_dev, _ = dec_query.shape
    dest = prompt_dest[:, 0]
    table = dest[:, None] == jnp.arange(n_ep, dtype=jnp.int32)[None, :]
    before = dot(strict_lower(ptok_dev), table.astype(jnp.bfloat16))
    rank = jnp.sum(jnp.where(table, before, 0.0), axis=1).astype(jnp.int32)
    target = dest * PEER_CAP + rank
    pick = (jnp.arange(n_ep * PEER_CAP, dtype=jnp.int32)[:, None] == target[None, :]).astype(
        jnp.bfloat16
    )
    tagged = jnp.concatenate(
        [prompt_latent, (prompt_slot + 1).astype(jnp.bfloat16)[:, None]], axis=1
    )
    send = dot(pick, tagged).astype(jnp.bfloat16).reshape(n_ep, PEER_CAP, width + 1)
    got = lax.all_to_all(send, "ep", split_axis=0, concat_axis=0, tiled=True)
    got = got.reshape(n_ep * PEER_CAP, width + 1)
    got_rows = got[:, :width]
    got_tags = got[:, width].astype(jnp.float32) - 1.0

    queries = dec_query.reshape(seq_dev, steps * heads_dev, width)
    old_scores = (
        jnp.einsum("sqw,skw->sqk", queries, old_cache, preferred_element_type=jnp.float32)
        * SCORE_SCALE
    )
    got_scores = (
        jnp.einsum("sqw,kw->sqk", queries, got_rows, preferred_element_type=jnp.float32)
        * SCORE_SCALE
    )
    new_scores = (
        jnp.einsum("sqw,skw->sqk", queries, new_latent, preferred_element_type=jnp.float32)
        * SCORE_SCALE
    )
    old_live = (
        jnp.arange(old_cache.shape[1], dtype=jnp.int32)[None, None, :] < cache_len[:, None, None]
    )
    got_live = got_tags[None, None, :] == jnp.arange(seq_dev, dtype=jnp.float32)[:, None, None]
    query_step = jnp.arange(steps * heads_dev, dtype=jnp.int32) // heads_dev
    new_live = jnp.arange(steps, dtype=jnp.int32)[None, None, :] <= query_step[None, :, None]
    old_scores = jnp.where(old_live, old_scores, -jnp.inf)
    got_scores = jnp.where(got_live, got_scores, -jnp.inf)
    new_scores = jnp.where(new_live, new_scores, -jnp.inf)
    top = jnp.maximum(
        jnp.maximum(jnp.max(old_scores, axis=2), jnp.max(got_scores, axis=2)),
        jnp.max(new_scores, axis=2),
    )[:, :, None]
    old_weights = jnp.exp(old_scores - top)
    got_weights = jnp.exp(got_scores - top)
    new_weights = jnp.exp(new_scores - top)
    total = (
        jnp.sum(old_weights, axis=2) + jnp.sum(got_weights, axis=2) + jnp.sum(new_weights, axis=2)
    )
    summed = jnp.einsum(
        "mpl,mlf->mpf",
        old_weights.astype(jnp.bfloat16),
        old_cache[:, :, :LAT],
        preferred_element_type=jnp.float32,
    )
    summed = summed + jnp.einsum(
        "sqk,kv->sqv",
        got_weights.astype(jnp.bfloat16),
        got_rows[:, :LAT],
        preferred_element_type=jnp.float32,
    )
    summed = summed + jnp.einsum(
        "mpl,mlf->mpf",
        new_weights.astype(jnp.bfloat16),
        new_latent[:, :, :LAT],
        preferred_element_type=jnp.float32,
    )
    return (summed / total[:, :, None]).astype(jnp.bfloat16).reshape(seq_dev, steps, heads_dev, LAT)


def experts(dec_states, moe_gain, expert_ids, route_weight, w_gate, w_up, w_down):
    seq_dev, steps, d_part = dec_states.shape
    tok = seq_dev * steps
    topk = expert_ids.shape[-1]
    me = lax.axis_index("ep")
    y = 2 * lax.axis_index("tp") + lax.axis_index("section")

    def part_of(k):
        return group_of_y((y + k) % NY)

    flat = dec_states.reshape(tok, d_part)
    wide = flat.astype(jnp.float32)
    squares = jnp.sum(wide * wide, axis=1, keepdims=True)
    meta = jnp.concatenate(
        [
            expert_ids.reshape(tok, topk).astype(jnp.float32),
            route_weight.reshape(tok, topk).astype(jnp.float32),
            squares,
        ],
        axis=1,
    )
    meta_z = jnp.concatenate([over_z(meta, k) for k in range(NZ)], axis=0)
    flat_z = jnp.concatenate([over_z(flat, k) for k in range(NZ)], axis=0)
    flat_2 = over_y(flat, 2)
    gain_2 = over_y(moe_gain, 2)
    flat_2z = jnp.concatenate([over_z(flat_2, k) for k in range(NZ)], axis=0)
    downs = [
        over_y(lax.dynamic_slice_in_dim(w_down[0], part_of(k) * d_part, d_part, axis=1), k)
        for k in range(NY)
    ]

    part_squares = meta_z[:, 2 * topk].reshape(NZ, tok)
    square_sum = part_squares
    for k in range(1, NY):
        square_sum = square_sum + over_y(part_squares, k)
    scale = lax.rsqrt(square_sum / (d_part * NY) + EPS).reshape(NZ * tok, 1)

    ids = meta_z[:, :topk].astype(jnp.int32)
    weight = meta_z[:, topk : 2 * topk]
    share = weight / jnp.sum(weight, axis=1, keepdims=True)
    turns = [(dx, dc) for dx in range(NX) for dc in range(NC)]
    here = jnp.stack(
        [me // 8 * 8 + (me // 2 + dx) % NX * 2 + (me % 2 + dc) % 2 for dx, dc in turns]
    ).astype(jnp.int32)
    named = ids[None, :, :] == here[:, None, None]
    names = jnp.any(named, axis=2)
    gives = jnp.sum(jnp.where(named, share[None, :, :], 0.0), axis=2)
    rank = dot(names.astype(jnp.bfloat16), strict_lower(NZ * tok).T)
    room = NZ * E_CAP
    slot = jnp.where(names, rank, -1.0)
    chosen = slot[:, None, :] == jnp.arange(room, dtype=jnp.float32)[None, :, None]
    pick = chosen.astype(jnp.bfloat16).reshape(len(turns) * room, NZ * tok)
    mix = jnp.where(chosen, gives[:, None, :], 0.0).reshape(len(turns) * room, NZ * tok)
    mix_high = mix.astype(jnp.bfloat16)
    mix_low = (mix - mix_high.astype(jnp.float32)).astype(jnp.bfloat16)

    def to_experts(states, gain):
        normed = (states.astype(jnp.float32) * scale * gain).astype(jnp.bfloat16)
        rows = dot(pick, normed).astype(jnp.bfloat16)
        return jnp.concatenate(
            [over_x(rows[j * room : (j + 1) * room], *turn) for j, turn in enumerate(turns)], axis=0
        )

    own = to_experts(flat_z, moe_gain)
    across = to_experts(flat_2z, gain_2)
    arrived = [(0, own), (2, across), (-1, over_y(own, 1)), (1, over_y(own, -1))]
    gate, up = 0.0, 0.0
    for k, rows in arrived:
        start = part_of(k % NY) * d_part
        gate = gate + dot(rows, lax.dynamic_slice_in_dim(w_gate[0], start, d_part, axis=0))
        up = up + dot(rows, lax.dynamic_slice_in_dim(w_up[0], start, d_part, axis=0))
    hidden = (jax.nn.silu(gate) * up).astype(jnp.bfloat16)
    out = 0.0
    for k in range(NY):
        out = out + dot(over_y(hidden, k), downs[k])
    out = out.astype(jnp.bfloat16)
    back = jnp.concatenate(
        [over_x(out[j * room : (j + 1) * room], -dx, dc) for j, (dx, dc) in enumerate(turns)],
        axis=0,
    )
    contract = (((0,), (0,)), ((), ()))
    mixed = lax.dot_general(mix_high, back, contract, preferred_element_type=jnp.float32)
    mixed = mixed + lax.dot_general(mix_low, back, contract, preferred_element_type=jnp.float32)
    mixed = mixed.astype(jnp.bfloat16)
    total = 0.0
    for k in range(NZ):
        total = total + over_z(mixed[k * tok : (k + 1) * tok], -k).astype(jnp.float32)
    return total.astype(jnp.bfloat16).reshape(seq_dev, steps, d_part)


def body(
    prompt_latent,
    prompt_dest,
    prompt_slot,
    old_cache,
    cache_len,
    new_latent,
    dec_query,
    dec_states,
    moe_gain,
    expert_ids,
    route_weight,
    w_gate,
    w_up,
    w_down,
):
    attn_out = attention(
        prompt_latent, prompt_dest, prompt_slot, old_cache, cache_len, new_latent, dec_query
    )
    moe_out = experts(dec_states, moe_gain, expert_ids, route_weight, w_gate, w_up, w_down)
    return (attn_out, moe_out)


def solution(mesh):
    placed = (
        P("ep", None),
        P("ep", None),
        P("ep"),
        P("ep", None, None),
        P("ep"),
        P("ep", None, None),
        P("ep", None, GROUP, None),
        P("ep", None, GROUP),
        P(GROUP),
        P("ep", None, None),
        P("ep", None, None),
        P("ep", None, GROUP),
        P("ep", None, GROUP),
        P("ep", GROUP, None),
    )
    return jax.shard_map(
        body,
        mesh=mesh,
        in_specs=placed,
        out_specs=(P("ep", None, GROUP, None), P("ep", None, GROUP)),
        check_vma=False,
    )
```

```python
import jax
import jax.numpy as jnp
from jax import lax
from jax.experimental import pallas as pl
from jax.experimental.pallas import tpu as pltpu
from jax.sharding import PartitionSpec as P

LAT = 512
EPS = 1e-06
SCORE_SCALE = 192.0 ** (-0.5)
NY = 4
ORDER = (0, 1, 3, 2)
E_CAP = 8
PEER_CAP = 4
CHUNKS = 2
SCOPED = 16 * 2**20
GROUP = ("section", "tp")


def group_of_y(y):
    return (y % 2) * 2 + (y // 2) % 2


def y_perm(k):
    return [(group_of_y(y), group_of_y((y + k) % NY)) for y in range(NY)]


def over_y(v, k):
    return lax.ppermute(v, GROUP, y_perm(k % NY)) if k % NY else v


def other_core(v):
    return lax.ppermute(v, "ep", [(i, i ^ 1) for i in range(lax.axis_size("ep"))])


def chips_exchange(v):
    n = lax.axis_size("ep")
    groups = [[i for i in range(n) if i % 2 == core] for core in range(2)]
    return lax.all_to_all(
        v, "ep", split_axis=0, concat_axis=0, tiled=True, axis_index_groups=groups
    )


def dot(a, b):
    return jnp.dot(a, b, preferred_element_type=jnp.float32)


def slots(names, half_tokens, cap):
    tokens = names.shape[1]
    i = jnp.arange(tokens, dtype=jnp.int32)
    own = i[:, None] // half_tokens == i[None, :] // half_tokens
    earlier = ((i[:, None] < i[None, :]) & own).astype(jnp.bfloat16)
    rank = dot(names.astype(jnp.bfloat16), earlier)
    side = i[None, :] // half_tokens == jnp.arange(2, dtype=jnp.int32)[:, None]
    slot = jnp.where(names[:, None, :] & side[None], rank[:, None, :], -1.0)
    return slot[:, :, None, :] == jnp.arange(cap, dtype=jnp.float32)[None, None, :, None]


def prompt_rows(prompt_latent, prompt_dest, prompt_slot, chips, core):
    ptok_dev, width = prompt_latent.shape
    tags = jnp.stack([prompt_slot + 1, prompt_dest[:, 0]], axis=1).astype(jnp.bfloat16)
    spare = jnp.zeros((ptok_dev, -(width + 2) % 128), jnp.bfloat16)
    tagged = jnp.concatenate([prompt_latent, tags, spare], axis=1)
    tagged = jnp.concatenate([tagged, other_core(tagged)], axis=0)
    dest = tagged[:, width + 1].astype(jnp.int32)
    owners = 2 * jnp.arange(chips, dtype=jnp.int32) + core
    chosen = slots(dest[None, :] == owners[:, None], ptok_dev, PEER_CAP)
    pick = chosen.astype(jnp.bfloat16).reshape(chips * 2 * PEER_CAP, 2 * ptok_dev)
    return dot(pick, tagged).astype(jnp.bfloat16)


WHOLE = pl.BlockSpec(memory_space=pltpu.VMEM)


def near_kernel(own, below, above, *refs):
    weights, out = refs[:-1], refs[-1]
    cols = weights[0].shape[1]
    gate, up = 0.0, 0.0
    for rows, gate_w, up_w in zip((own, below, above), weights[0::2], weights[1::2]):
        gate = gate + dot(rows[...], gate_w[...])
        up = up + dot(rows[...], up_w[...])
    out[:, :cols] = gate
    out[:, cols:] = up


def near_sums(own, below, above, weights):
    n, depth = own.shape
    cols = weights[0].shape[1]
    return pl.pallas_call(
        near_kernel,
        out_shape=jax.ShapeDtypeStruct((n, 2 * cols), jnp.float32),
        in_specs=[WHOLE] * (3 + len(weights)),
        out_specs=WHOLE,
        compiler_params=pltpu.CompilerParams(vmem_limit_bytes=SCOPED),
        cost_estimate=pl.CostEstimate(
            flops=12 * n * depth * cols, bytes_accessed=12 * depth * cols, transcendentals=0
        ),
        name="near_sums",
    )(own, below, above, *weights)


def hidden_kernel(low, high, sums, gate_w, up_w, out):
    n, cols = out.shape
    mid = n // 2
    for rows, first in ((low, 0), (high, mid)):
        at = slice(first, first + mid)
        gate = sums[at, :cols] + dot(rows[...], gate_w[...])
        up = sums[at, cols:] + dot(rows[...], up_w[...])
        out[at, :] = (gate / (1.0 + jnp.exp(-gate)) * up).astype(out.dtype)


def hidden_units(low, high, sums, gate_w, up_w):
    mid, depth = low.shape
    cols = gate_w.shape[1]
    return pl.pallas_call(
        hidden_kernel,
        out_shape=jax.ShapeDtypeStruct((2 * mid, cols), jnp.bfloat16),
        in_specs=[WHOLE] * 5,
        out_specs=WHOLE,
        compiler_params=pltpu.CompilerParams(vmem_limit_bytes=SCOPED),
        cost_estimate=pl.CostEstimate(
            flops=8 * mid * depth * cols,
            bytes_accessed=4 * depth * cols,
            transcendentals=2 * mid * cols,
        ),
        name="hidden_units",
    )(low, high, sums, gate_w, up_w)


def down_kernel(n_hidden, n_downs, *refs):
    hidden, downs = refs[:n_hidden], refs[n_hidden : n_hidden + n_downs]
    out = refs[-1]
    depth, cols = downs[0].shape
    tile = 256 if cols % 256 == 0 else 128

    @pl.loop(0, cols // tile)
    def _(step):
        at = pl.ds(pl.multiple_of(step * tile, tile), tile)
        total = 0.0
        for k, w in enumerate(downs[:-2]):
            total = total + dot(hidden[k][...], w[:depth, at])
        rows = 0
        for w in downs[-2:]:
            total = total + dot(hidden[-1][:, rows : rows + w.shape[0]], w[:, at])
            rows += w.shape[0]
        out[:, at] = total.astype(out.dtype)

    if len(refs) > n_hidden + n_downs + 1:
        out[:, cols:] = refs[-2][...]


def down_product(hidden, downs, rider=None):
    n, depth = hidden[0].shape
    cols = downs[0].shape[1]
    more = [] if rider is None else [rider]
    return pl.pallas_call(
        lambda *refs: down_kernel(len(hidden), len(downs), *refs),
        out_shape=jax.ShapeDtypeStruct(
            (n, cols + sum(v.shape[1] for v in more)), jnp.bfloat16
        ),
        in_specs=[WHOLE] * (len(hidden) + len(downs) + len(more)),
        out_specs=WHOLE,
        compiler_params=pltpu.CompilerParams(vmem_limit_bytes=SCOPED),
        cost_estimate=pl.CostEstimate(
            flops=2 * n * depth * cols * len(hidden),
            bytes_accessed=2 * depth * cols * len(hidden),
            transcendentals=0,
        ),
        name="down_product",
    )(*hidden, *downs, *more)


def attention(got, old_cache, cache_len, new_latent, dec_query):
    seq_dev, steps, heads_dev, width = dec_query.shape
    got_rows = got[:, :width]
    got_tags = got[:, width].astype(jnp.float32) - 1.0
    queries = dec_query.reshape(seq_dev, steps * heads_dev, width)
    old_scores = (
        jnp.einsum("sqw,skw->sqk", queries, old_cache, preferred_element_type=jnp.float32)
        * SCORE_SCALE
    )
    got_scores = (
        jnp.einsum("sqw,kw->sqk", queries, got_rows, preferred_element_type=jnp.float32)
        * SCORE_SCALE
    )
    new_scores = (
        jnp.einsum("sqw,skw->sqk", queries, new_latent, preferred_element_type=jnp.float32)
        * SCORE_SCALE
    )
    old_live = (
        jnp.arange(old_cache.shape[1], dtype=jnp.int32)[None, None, :] < cache_len[:, None, None]
    )
    got_live = got_tags[None, None, :] == jnp.arange(seq_dev, dtype=jnp.float32)[:, None, None]
    query_step = jnp.arange(steps * heads_dev, dtype=jnp.int32) // heads_dev
    new_live = jnp.arange(steps, dtype=jnp.int32)[None, None, :] <= query_step[None, :, None]
    old_scores = jnp.where(old_live, old_scores, -jnp.inf)
    got_scores = jnp.where(got_live, got_scores, -jnp.inf)
    new_scores = jnp.where(new_live, new_scores, -jnp.inf)
    top = jnp.maximum(
        jnp.maximum(jnp.max(old_scores, axis=2), jnp.max(got_scores, axis=2)),
        jnp.max(new_scores, axis=2),
    )[:, :, None]
    old_weights = jnp.exp(old_scores - top)
    got_weights = jnp.exp(got_scores - top)
    new_weights = jnp.exp(new_scores - top)
    total = (
        jnp.sum(old_weights, axis=2) + jnp.sum(got_weights, axis=2) + jnp.sum(new_weights, axis=2)
    )
    summed = jnp.einsum(
        "mpl,mlf->mpf",
        old_weights.astype(jnp.bfloat16),
        old_cache[:, :, :LAT],
        preferred_element_type=jnp.float32,
    )
    summed = summed + jnp.einsum(
        "sqk,kv->sqv",
        got_weights.astype(jnp.bfloat16),
        got_rows[:, :LAT],
        preferred_element_type=jnp.float32,
    )
    summed = summed + jnp.einsum(
        "mpl,mlf->mpf",
        new_weights.astype(jnp.bfloat16),
        new_latent[:, :, :LAT],
        preferred_element_type=jnp.float32,
    )
    return (summed / total[:, :, None]).astype(jnp.bfloat16).reshape(seq_dev, steps, heads_dev, LAT)


def experts(dec_states, moe_gain, expert_ids, route_weight, w_gate, w_up, w_down, prompts, attend):
    seq_dev, steps, d_part = dec_states.shape
    tok = seq_dev * steps
    topk = expert_ids.shape[-1]
    chips = lax.axis_size("ep") // 2
    core = lax.axis_index("ep") % 2
    y = 2 * lax.axis_index("tp") + lax.axis_index("section")

    def part_of(k):
        return group_of_y((y + k) % NY)

    wide = dec_states.reshape(tok, d_part).astype(jnp.float32)
    squares = jnp.sum(wide * wide, axis=1)
    square_sum = squares
    for k in range(1, NY):
        square_sum = square_sum + over_y(squares, k)
    scale = lax.rsqrt(square_sum / (d_part * NY) + EPS)[:, None]
    normed = (wide * scale * moe_gain).astype(jnp.bfloat16)
    kept, upward, downward, across = [
        lax.dynamic_slice_in_dim(w_down[0], part_of(k) * d_part, d_part, axis=1) for k in ORDER
    ]
    units = across.shape[0]
    upward = jnp.concatenate([upward, across[: units // 2]], axis=0)
    downward = jnp.concatenate([downward, across[units // 2 :]], axis=0)
    upward, downward = over_y(upward, 1), over_y(downward, -1)
    downs = [kept, upward, downward, over_y(upward[units:], 1), over_y(downward[units:], -1)]
    meta = jnp.concatenate(
        [expert_ids.reshape(tok, topk), route_weight.reshape(tok, topk)], axis=1
    ).astype(jnp.float32)
    meta = jnp.concatenate([meta, other_core(meta)], axis=0)
    normed = jnp.concatenate([normed, other_core(normed)], axis=0)
    ids = meta[:, :topk].astype(jnp.int32)
    here = 2 * jnp.arange(chips, dtype=jnp.int32) + core
    named = ids.T[:, None, :] == here[None, :, None]
    chosen = slots(jnp.any(named, axis=0), tok, E_CAP)
    half = E_CAP // CHUNKS
    n = chips * 2 * half
    chosen = [chosen[:, :, c * half : (c + 1) * half] for c in range(CHUNKS)]
    picks = [v.astype(jnp.bfloat16).reshape(n, 2 * tok) for v in chosen]

    def exchange(v):
        return chips_exchange(v.reshape(chips, 2 * half, -1)).reshape(n, -1)

    sends = [dot(pick, normed).astype(jnp.bfloat16) for pick in picks]
    first = exchange(sends[0])
    first, second, gate_w, up_w = lax.optimization_barrier(
        (first, sends[1], w_gate[0], w_up[0])
    )
    blocks = [
        lax.dynamic_slice_in_dim(source, part_of(k) * d_part, d_part, axis=0)
        for k in (0, NY - 1, 1, 2)
        for source in (gate_w, up_w)
    ]
    arrived = [first, exchange(second)]

    def neighbours(rows):
        return over_y(rows, 1), over_y(rows, -1)

    near = [neighbours(rows) for rows in arrived]

    weight = meta[:, topk : 2 * topk]
    share = weight / jnp.sum(weight, axis=1, keepdims=True)
    gives = jnp.sum(jnp.where(named, share.T[:, None, :], 0.0), axis=0)
    mixes = []
    for v in chosen:
        mix = jnp.where(v, gives[:, None, None, :], 0.0).reshape(n, 2 * tok)
        high = lax.reduce_precision(mix, 8, 7)
        mixes.append([high.astype(jnp.bfloat16), (mix - high).astype(jnp.bfloat16)])
    mixed = 0.0
    contract = (((0,), (0,)), ((), ()))
    for c in range(CHUNKS):
        below, above = near[c]
        if c == 0:
            below, above, downs, blocks = lax.optimization_barrier((below, above, downs, blocks))
        mid = n // 2
        low, high = over_y(below[:mid], 1), over_y(above[mid:], -1)
        sums = near_sums(arrived[c], below, above, blocks[:6])
        hidden = hidden_units(low, high, sums, *blocks[6:])
        hidden = [over_y(hidden, k) for k in ORDER]
        out = down_product(hidden, downs, prompts if c == 0 else None)
        if c == 0:
            out, *near[1] = lax.optimization_barrier((out, *near[1]))
        back = exchange(out)
        if c == 0:
            attn_out = attend(back[:, d_part:])
        else:
            back, attn_out, mixed, mixes = lax.optimization_barrier((back, attn_out, mixed, mixes))
        for part in mixes[c]:
            mixed = mixed + lax.dot_general(
                part, back[:, :d_part], contract, preferred_element_type=jnp.float32
            )
    mixed = mixed[:tok] + other_core(mixed[tok:].astype(jnp.bfloat16)).astype(jnp.float32)
    return mixed.astype(jnp.bfloat16).reshape(seq_dev, steps, d_part), attn_out


def body(
    prompt_latent,
    prompt_dest,
    prompt_slot,
    old_cache,
    cache_len,
    new_latent,
    dec_query,
    dec_states,
    moe_gain,
    expert_ids,
    route_weight,
    w_gate,
    w_up,
    w_down,
):
    ep_index, n_ep = lax.axis_index("ep"), lax.axis_size("ep")
    prompts = prompt_rows(prompt_latent, prompt_dest, prompt_slot, n_ep // 2, ep_index % 2)

    def attend(got):
        return attention(got, old_cache, cache_len, new_latent, dec_query)

    moe_out, attn_out = experts(
        dec_states, moe_gain, expert_ids, route_weight, w_gate, w_up, w_down, prompts, attend
    )
    return (attn_out, moe_out)


def solution(mesh):
    placed = (
        P("ep", None),
        P("ep", None),
        P("ep"),
        P("ep", None, None),
        P("ep"),
        P("ep", None, None),
        P("ep", None, GROUP, None),
        P("ep", None, GROUP),
        P(GROUP),
        P("ep", None, None),
        P("ep", None, None),
        P("ep", None, GROUP),
        P("ep", None, GROUP),
        P("ep", GROUP, None),
    )
    return jax.shard_map(
        body,
        mesh=mesh,
        in_specs=placed,
        out_specs=(P("ep", None, GROUP, None), P("ep", None, GROUP)),
        check_vma=False,
    )
```

```python
import jax
import jax.numpy as jnp
from jax import lax
from jax.experimental import pallas as pl
from jax.experimental.pallas import tpu as pltpu
from jax.sharding import PartitionSpec as P

LAT = 512
EPS = 1e-06
SCORE_SCALE = 192.0 ** (-0.5)
NY = 4
ORDER = (0, 1, 3, 2)
E_CAP = 8
PEER_CAP = 4
CHUNKS = 2
SCOPED = 16 * 2**20
GROUP = ("section", "tp")


def group_of_y(y):
    return (y % 2) * 2 + (y // 2) % 2


def y_perm(k):
    return [(group_of_y(y), group_of_y((y + k) % NY)) for y in range(NY)]


def over_y(v, k):
    return lax.ppermute(v, GROUP, y_perm(k % NY)) if k % NY else v


def other_core(v):
    return lax.ppermute(v, "ep", [(i, i ^ 1) for i in range(lax.axis_size("ep"))])


def chips_exchange(v):
    n = lax.axis_size("ep")
    groups = [[i for i in range(n) if i % 2 == core] for core in range(2)]
    return lax.all_to_all(
        v, "ep", split_axis=0, concat_axis=0, tiled=True, axis_index_groups=groups
    )


def dot(a, b):
    return jnp.dot(a, b, preferred_element_type=jnp.float32)


def slots(names, half_tokens, cap):
    tokens = names.shape[1]
    i = jnp.arange(tokens, dtype=jnp.int32)
    own = i[:, None] // half_tokens == i[None, :] // half_tokens
    earlier = ((i[:, None] < i[None, :]) & own).astype(jnp.bfloat16)
    rank = dot(names.astype(jnp.bfloat16), earlier)
    side = i[None, :] // half_tokens == jnp.arange(2, dtype=jnp.int32)[:, None]
    slot = jnp.where(names[:, None, :] & side[None], rank[:, None, :], -1.0)
    return slot[:, :, None, :] == jnp.arange(cap, dtype=jnp.float32)[None, None, :, None]


def prompt_rows(prompt_latent, prompt_dest, prompt_slot, chips, core):
    ptok_dev, width = prompt_latent.shape
    tags = jnp.stack([prompt_slot + 1, prompt_dest[:, 0]], axis=1).astype(jnp.bfloat16)
    spare = jnp.zeros((ptok_dev, -(width + 2) % 128), jnp.bfloat16)
    tagged = jnp.concatenate([prompt_latent, tags, spare], axis=1)
    tagged = jnp.concatenate([tagged, other_core(tagged)], axis=0)
    dest = tagged[:, width + 1].astype(jnp.int32)
    owners = 2 * jnp.arange(chips, dtype=jnp.int32) + core
    chosen = slots(dest[None, :] == owners[:, None], ptok_dev, PEER_CAP)
    pick = chosen.astype(jnp.bfloat16).reshape(chips * 2 * PEER_CAP, 2 * ptok_dev)
    return dot(pick, tagged).astype(jnp.bfloat16)


WHOLE = pl.BlockSpec(memory_space=pltpu.VMEM)


def near_kernel(own, below, above, *refs):
    weights, out = refs[:-1], refs[-1]
    cols = weights[0].shape[1]
    gate, up = 0.0, 0.0
    for rows, gate_w, up_w in zip((own, below, above), weights[0::2], weights[1::2]):
        gate = gate + dot(rows[...], gate_w[...])
        up = up + dot(rows[...], up_w[...])
    out[:, :cols] = gate
    out[:, cols:] = up


def near_sums(own, below, above, weights):
    n, depth = own.shape
    cols = weights[0].shape[1]
    return pl.pallas_call(
        near_kernel,
        out_shape=jax.ShapeDtypeStruct((n, 2 * cols), jnp.float32),
        in_specs=[WHOLE] * (3 + len(weights)),
        out_specs=WHOLE,
        compiler_params=pltpu.CompilerParams(vmem_limit_bytes=SCOPED),
        cost_estimate=pl.CostEstimate(
            flops=12 * n * depth * cols, bytes_accessed=12 * depth * cols, transcendentals=0
        ),
        name="near_sums",
    )(own, below, above, *weights)


def hidden_kernel(low, high, sums, factor, gate_w, up_w, out):
    n, cols = out.shape
    mid = n // 2
    for rows, first in ((low, 0), (high, mid)):
        at = slice(first, first + mid)
        gate = sums[at, :cols] + dot(rows[...], gate_w[...])
        up = sums[at, cols:] + dot(rows[...], up_w[...])
        gate, up = gate * factor[at, :], up * factor[at, :]
        out[at, :] = (gate / (1.0 + jnp.exp(-gate)) * up).astype(out.dtype)


def hidden_units(low, high, sums, factor, gate_w, up_w):
    mid, depth = low.shape
    cols = gate_w.shape[1]
    return pl.pallas_call(
        hidden_kernel,
        out_shape=jax.ShapeDtypeStruct((2 * mid, cols), jnp.bfloat16),
        in_specs=[WHOLE] * 6,
        out_specs=WHOLE,
        compiler_params=pltpu.CompilerParams(vmem_limit_bytes=SCOPED),
        cost_estimate=pl.CostEstimate(
            flops=8 * mid * depth * cols,
            bytes_accessed=4 * depth * cols,
            transcendentals=2 * mid * cols,
        ),
        name="hidden_units",
    )(low, high, sums, factor, gate_w, up_w)


def down_kernel(n_hidden, n_downs, *refs):
    hidden, downs = refs[:n_hidden], refs[n_hidden : n_hidden + n_downs]
    out = refs[-1]
    cols = downs[0].shape[1]
    tile = 256 if cols % 256 == 0 else 128

    @pl.loop(0, cols // tile)
    def _(step):
        at = pl.ds(pl.multiple_of(step * tile, tile), tile)
        total = 0.0
        for h, w in zip(hidden, downs):
            total = total + dot(h[...], w[:, at])
        out[:, at] = total.astype(out.dtype)


def down_product(hidden, downs):
    n, depth = hidden[0].shape
    cols = downs[0].shape[1]
    return pl.pallas_call(
        lambda *refs: down_kernel(len(hidden), len(downs), *refs),
        out_shape=jax.ShapeDtypeStruct((n, cols), jnp.bfloat16),
        in_specs=[WHOLE] * (len(hidden) + len(downs)),
        out_specs=WHOLE,
        compiler_params=pltpu.CompilerParams(vmem_limit_bytes=SCOPED),
        cost_estimate=pl.CostEstimate(
            flops=2 * n * depth * cols * len(hidden),
            bytes_accessed=2 * depth * cols * len(hidden),
            transcendentals=0,
        ),
        name="down_product",
    )(*hidden, *downs)


def attention(got, old_cache, cache_len, new_latent, dec_query):
    seq_dev, steps, heads_dev, width = dec_query.shape
    got_rows = got[:, :width]
    got_tags = got[:, width].astype(jnp.float32) - 1.0
    queries = dec_query.reshape(seq_dev, steps * heads_dev, width)
    old_scores = (
        jnp.einsum("sqw,skw->sqk", queries, old_cache, preferred_element_type=jnp.float32)
        * SCORE_SCALE
    )
    got_scores = (
        jnp.einsum("sqw,kw->sqk", queries, got_rows, preferred_element_type=jnp.float32)
        * SCORE_SCALE
    )
    new_scores = (
        jnp.einsum("sqw,skw->sqk", queries, new_latent, preferred_element_type=jnp.float32)
        * SCORE_SCALE
    )
    old_live = (
        jnp.arange(old_cache.shape[1], dtype=jnp.int32)[None, None, :] < cache_len[:, None, None]
    )
    got_live = got_tags[None, None, :] == jnp.arange(seq_dev, dtype=jnp.float32)[:, None, None]
    query_step = jnp.arange(steps * heads_dev, dtype=jnp.int32) // heads_dev
    new_live = jnp.arange(steps, dtype=jnp.int32)[None, None, :] <= query_step[None, :, None]
    old_scores = jnp.where(old_live, old_scores, -jnp.inf)
    got_scores = jnp.where(got_live, got_scores, -jnp.inf)
    new_scores = jnp.where(new_live, new_scores, -jnp.inf)
    top = jnp.maximum(
        jnp.maximum(jnp.max(old_scores, axis=2), jnp.max(got_scores, axis=2)),
        jnp.max(new_scores, axis=2),
    )[:, :, None]
    old_weights = jnp.exp(old_scores - top)
    got_weights = jnp.exp(got_scores - top)
    new_weights = jnp.exp(new_scores - top)
    total = (
        jnp.sum(old_weights, axis=2) + jnp.sum(got_weights, axis=2) + jnp.sum(new_weights, axis=2)
    )
    summed = jnp.einsum(
        "mpl,mlf->mpf",
        old_weights.astype(jnp.bfloat16),
        old_cache[:, :, :LAT],
        preferred_element_type=jnp.float32,
    )
    summed = summed + jnp.einsum(
        "sqk,kv->sqv",
        got_weights.astype(jnp.bfloat16),
        got_rows[:, :LAT],
        preferred_element_type=jnp.float32,
    )
    summed = summed + jnp.einsum(
        "mpl,mlf->mpf",
        new_weights.astype(jnp.bfloat16),
        new_latent[:, :, :LAT],
        preferred_element_type=jnp.float32,
    )
    return (summed / total[:, :, None]).astype(jnp.bfloat16).reshape(seq_dev, steps, heads_dev, LAT)


def experts(dec_states, moe_gain, expert_ids, route_weight, w_gate, w_up, w_down, prompts, attend):
    seq_dev, steps, d_part = dec_states.shape
    tok = seq_dev * steps
    topk = expert_ids.shape[-1]
    chips = lax.axis_size("ep") // 2
    core = lax.axis_index("ep") % 2
    y = 2 * lax.axis_index("tp") + lax.axis_index("section")

    def part_of(k):
        return group_of_y((y + k) % NY)

    wide = dec_states.reshape(tok, d_part).astype(jnp.float32)
    scaled = (wide * moe_gain).astype(jnp.bfloat16)
    meta = jnp.concatenate(
        [
            expert_ids.reshape(tok, topk).astype(jnp.float32),
            route_weight.reshape(tok, topk).astype(jnp.float32),
            jnp.sum(wide * wide, axis=1, keepdims=True),
        ],
        axis=1,
    )
    meta = jnp.concatenate([meta, other_core(meta)], axis=0)
    scaled = jnp.concatenate([scaled, other_core(scaled)], axis=0)
    downs = [
        over_y(lax.dynamic_slice_in_dim(w_down[0], part_of(k) * d_part, d_part, axis=1), k)
        for k in ORDER
    ]
    ids = meta[:, :topk].astype(jnp.int32)
    here = 2 * jnp.arange(chips, dtype=jnp.int32) + core
    named = ids.T[:, None, :] == here[None, :, None]
    chosen = slots(jnp.any(named, axis=0), tok, E_CAP)
    half = E_CAP // CHUNKS
    n = chips * 2 * half
    chosen = [chosen[:, :, c * half : (c + 1) * half] for c in range(CHUNKS)]
    pick = jnp.stack(chosen, axis=1).astype(jnp.bfloat16).reshape(CHUNKS * n, 2 * tok)

    def exchange(v):
        return chips_exchange(v.reshape(chips, v.shape[0] // chips, -1))

    rows = exchange(dot(pick, scaled).astype(jnp.bfloat16))
    squares = meta[:, 2 * topk]
    square_sum = squares
    for k in range(1, NY):
        square_sum = square_sum + over_y(squares, k)
    scale = lax.rsqrt(square_sum / (d_part * NY) + EPS)
    pieces, rest = [], scale
    for _ in range(3):
        pieces.append(lax.reduce_precision(rest, 8, 7))
        rest = rest - pieces[-1]
    pieces = jnp.stack(pieces, axis=1).astype(jnp.bfloat16)
    scales = jnp.concatenate(
        [dot(v.astype(jnp.bfloat16).reshape(n, 2 * tok), pieces) for v in chosen], axis=1
    ).astype(jnp.bfloat16)
    follow = jnp.concatenate([prompts[:, : -scales.shape[1]], scales], axis=1)
    rows, downs, follow, gate_w, up_w = lax.optimization_barrier(
        (rows, downs, follow, w_gate[0], w_up[0])
    )
    got = exchange(follow).reshape(n, -1)
    attn_out = attend(got)
    factors = [
        jnp.sum(got[:, at : at + 3].astype(jnp.float32), axis=1, keepdims=True)
        for at in (got.shape[1] - 6, got.shape[1] - 3)
    ]
    blocks = [
        lax.dynamic_slice_in_dim(source, part_of(k) * d_part, d_part, axis=0)
        for k in (0, NY - 1, 1, 2)
        for source in (gate_w, up_w)
    ]
    arrived = [
        rows[:, c * 2 * half : (c + 1) * 2 * half].reshape(n, d_part) for c in range(CHUNKS)
    ]

    def neighbours(rows):
        return over_y(rows, 1), over_y(rows, -1)

    def across(below, above):
        mid = n // 2
        return over_y(below[:mid], 1), over_y(above[mid:], -1)

    near = [neighbours(arrived[0])]
    near[0], arrived[1], blocks = lax.optimization_barrier((near[0], arrived[1], blocks))
    near.append(neighbours(arrived[1]))
    far = [across(*v) for v in near]

    weight = meta[:, topk : 2 * topk]
    share = weight / jnp.sum(weight, axis=1, keepdims=True)
    gives = jnp.sum(jnp.where(named, share.T[:, None, :], 0.0), axis=0)
    mixes = []
    for v in chosen:
        mix = jnp.where(v, gives[:, None, None, :], 0.0).reshape(n, 2 * tok)
        high = lax.reduce_precision(mix, 8, 7)
        mixes.append([high.astype(jnp.bfloat16), (mix - high).astype(jnp.bfloat16)])
    mixed = 0.0
    contract = (((0,), (0,)), ((), ()))
    for c in range(CHUNKS):
        below, above = near[c]
        low, high = far[c]
        sums = near_sums(arrived[c], below, above, blocks[:6])
        hidden = hidden_units(low, high, sums, factors[c], *blocks[6:])
        hidden = [over_y(hidden, k) for k in ORDER]
        out = down_product(hidden, downs)
        if c == 0:
            out, near[1], far[1] = lax.optimization_barrier((out, near[1], far[1]))
        back = exchange(out).reshape(n, -1)
        if c == 1:
            back, attn_out, mixed, mixes = lax.optimization_barrier((back, attn_out, mixed, mixes))
        for part in mixes[c]:
            mixed = mixed + lax.dot_general(
                part, back, contract, preferred_element_type=jnp.float32
            )
    mixed = mixed[:tok] + other_core(mixed[tok:].astype(jnp.bfloat16)).astype(jnp.float32)
    return mixed.astype(jnp.bfloat16).reshape(seq_dev, steps, d_part), attn_out


def body(
    prompt_latent,
    prompt_dest,
    prompt_slot,
    old_cache,
    cache_len,
    new_latent,
    dec_query,
    dec_states,
    moe_gain,
    expert_ids,
    route_weight,
    w_gate,
    w_up,
    w_down,
):
    ep_index, n_ep = lax.axis_index("ep"), lax.axis_size("ep")
    prompts = prompt_rows(prompt_latent, prompt_dest, prompt_slot, n_ep // 2, ep_index % 2)

    def attend(got):
        return attention(got, old_cache, cache_len, new_latent, dec_query)

    moe_out, attn_out = experts(
        dec_states, moe_gain, expert_ids, route_weight, w_gate, w_up, w_down, prompts, attend
    )
    return (attn_out, moe_out)


def solution(mesh):
    placed = (
        P("ep", None),
        P("ep", None),
        P("ep"),
        P("ep", None, None),
        P("ep"),
        P("ep", None, None),
        P("ep", None, GROUP, None),
        P("ep", None, GROUP),
        P(GROUP),
        P("ep", None, None),
        P("ep", None, None),
        P("ep", None, GROUP),
        P("ep", None, GROUP),
        P("ep", GROUP, None),
    )
    return jax.shard_map(
        body,
        mesh=mesh,
        in_specs=placed,
        out_specs=(P("ep", None, GROUP, None), P("ep", None, GROUP)),
        check_vma=False,
    )
```

```python
import jax
import jax.numpy as jnp
from jax import lax
from jax.experimental import pallas as pl
from jax.experimental.pallas import tpu as pltpu
from jax.sharding import PartitionSpec as P

LAT = 512
EPS = 1e-06
SCORE_SCALE = 192.0 ** (-0.5)
NY = 4
ORDER = (0, 1, 3, 2)
E_CAP = 8
PEER_CAP = 4
CHUNKS = 2
SCOPED = 16 * 2**20
GROUP = ("section", "tp")


def group_of_y(y):
    return (y % 2) * 2 + (y // 2) % 2


def y_perm(k):
    return [(group_of_y(y), group_of_y((y + k) % NY)) for y in range(NY)]


def over_y(v, k):
    return lax.ppermute(v, GROUP, y_perm(k % NY)) if k % NY else v


def other_core(v):
    return lax.ppermute(v, "ep", [(i, i ^ 1) for i in range(lax.axis_size("ep"))])


def chips_exchange(v):
    n = lax.axis_size("ep")
    groups = [[i for i in range(n) if i % 2 == core] for core in range(2)]
    return lax.all_to_all(
        v, "ep", split_axis=0, concat_axis=0, tiled=True, axis_index_groups=groups
    )


def dot(a, b):
    return jnp.dot(a, b, preferred_element_type=jnp.float32)


def slots(names, half_tokens, cap):
    tokens = names.shape[1]
    i = jnp.arange(tokens, dtype=jnp.int32)
    own = i[:, None] // half_tokens == i[None, :] // half_tokens
    earlier = ((i[:, None] < i[None, :]) & own).astype(jnp.bfloat16)
    rank = dot(names.astype(jnp.bfloat16), earlier)
    side = i[None, :] // half_tokens == jnp.arange(2, dtype=jnp.int32)[:, None]
    slot = jnp.where(names[:, None, :] & side[None], rank[:, None, :], -1.0)
    return slot[:, :, None, :] == jnp.arange(cap, dtype=jnp.float32)[None, None, :, None]


def prompt_rows(prompt_latent, prompt_dest, prompt_slot, chips, core):
    ptok_dev, width = prompt_latent.shape
    tags = jnp.stack([prompt_slot + 1, prompt_dest[:, 0]], axis=1).astype(jnp.bfloat16)
    spare = jnp.zeros((ptok_dev, -(width + 2) % 128), jnp.bfloat16)
    tagged = jnp.concatenate([prompt_latent, tags, spare], axis=1)
    tagged = jnp.concatenate([tagged, other_core(tagged)], axis=0)
    dest = tagged[:, width + 1].astype(jnp.int32)
    owners = 2 * jnp.arange(chips, dtype=jnp.int32) + core
    chosen = slots(dest[None, :] == owners[:, None], ptok_dev, PEER_CAP)
    pick = chosen.astype(jnp.bfloat16).reshape(chips * 2 * PEER_CAP, 2 * ptok_dev)
    return dot(pick, tagged).astype(jnp.bfloat16)


WHOLE = pl.BlockSpec(memory_space=pltpu.VMEM)


def near_kernel(own, below, above, *refs):
    weights, out = refs[:-1], refs[-1]
    cols = weights[0].shape[1]
    gate, up = 0.0, 0.0
    for rows, gate_w, up_w in zip((own, below, above), weights[0::2], weights[1::2]):
        gate = gate + dot(rows[...], gate_w[...])
        up = up + dot(rows[...], up_w[...])
    out[:, :cols] = gate
    out[:, cols:] = up


def near_sums(own, below, above, weights):
    n, depth = own.shape
    cols = weights[0].shape[1]
    return pl.pallas_call(
        near_kernel,
        out_shape=jax.ShapeDtypeStruct((n, 2 * cols), jnp.float32),
        in_specs=[WHOLE] * (3 + len(weights)),
        out_specs=WHOLE,
        compiler_params=pltpu.CompilerParams(vmem_limit_bytes=SCOPED),
        cost_estimate=pl.CostEstimate(
            flops=12 * n * depth * cols, bytes_accessed=12 * depth * cols, transcendentals=0
        ),
        name="near_sums",
    )(own, below, above, *weights)


def hidden_kernel(low, high, sums, factor, gate_w, up_w, out):
    n, cols = out.shape
    mid = n // 2
    for rows, first in ((low, 0), (high, mid)):
        at = slice(first, first + mid)
        gate = sums[at, :cols] + dot(rows[...], gate_w[...])
        up = sums[at, cols:] + dot(rows[...], up_w[...])
        gate, up = gate * factor[at, :], up * factor[at, :]
        out[at, :] = (gate / (1.0 + jnp.exp(-gate)) * up).astype(out.dtype)


def hidden_units(low, high, sums, factor, gate_w, up_w):
    mid, depth = low.shape
    cols = gate_w.shape[1]
    return pl.pallas_call(
        hidden_kernel,
        out_shape=jax.ShapeDtypeStruct((2 * mid, cols), jnp.bfloat16),
        in_specs=[WHOLE] * 6,
        out_specs=WHOLE,
        compiler_params=pltpu.CompilerParams(vmem_limit_bytes=SCOPED),
        cost_estimate=pl.CostEstimate(
            flops=8 * mid * depth * cols,
            bytes_accessed=4 * depth * cols,
            transcendentals=2 * mid * cols,
        ),
        name="hidden_units",
    )(low, high, sums, factor, gate_w, up_w)


def down_kernel(n_hidden, n_downs, *refs):
    hidden, downs = refs[:n_hidden], refs[n_hidden : n_hidden + n_downs]
    out = refs[-1]
    cols = downs[0].shape[1]
    tile = 256 if cols % 256 == 0 else 128

    @pl.loop(0, cols // tile)
    def _(step):
        at = pl.ds(pl.multiple_of(step * tile, tile), tile)
        total = 0.0
        for h, w in zip(hidden, downs):
            total = total + dot(h[...], w[:, at])
        out[:, at] = total.astype(out.dtype)


def down_product(hidden, downs):
    n, depth = hidden[0].shape
    cols = downs[0].shape[1]
    return pl.pallas_call(
        lambda *refs: down_kernel(len(hidden), len(downs), *refs),
        out_shape=jax.ShapeDtypeStruct((n, cols), jnp.bfloat16),
        in_specs=[WHOLE] * (len(hidden) + len(downs)),
        out_specs=WHOLE,
        compiler_params=pltpu.CompilerParams(vmem_limit_bytes=SCOPED),
        cost_estimate=pl.CostEstimate(
            flops=2 * n * depth * cols * len(hidden),
            bytes_accessed=2 * depth * cols * len(hidden),
            transcendentals=0,
        ),
        name="down_product",
    )(*hidden, *downs)


def attention(got, old_cache, cache_len, new_latent, dec_query):
    seq_dev, steps, heads_dev, width = dec_query.shape
    got_rows = got[:, :width]
    got_tags = got[:, width].astype(jnp.float32) - 1.0
    queries = dec_query.reshape(seq_dev, steps * heads_dev, width)
    old_scores = (
        jnp.einsum("sqw,skw->sqk", queries, old_cache, preferred_element_type=jnp.float32)
        * SCORE_SCALE
    )
    got_scores = (
        jnp.einsum("sqw,kw->sqk", queries, got_rows, preferred_element_type=jnp.float32)
        * SCORE_SCALE
    )
    new_scores = (
        jnp.einsum("sqw,skw->sqk", queries, new_latent, preferred_element_type=jnp.float32)
        * SCORE_SCALE
    )
    old_live = (
        jnp.arange(old_cache.shape[1], dtype=jnp.int32)[None, None, :] < cache_len[:, None, None]
    )
    got_live = got_tags[None, None, :] == jnp.arange(seq_dev, dtype=jnp.float32)[:, None, None]
    query_step = jnp.arange(steps * heads_dev, dtype=jnp.int32) // heads_dev
    new_live = jnp.arange(steps, dtype=jnp.int32)[None, None, :] <= query_step[None, :, None]
    old_scores = jnp.where(old_live, old_scores, -jnp.inf)
    got_scores = jnp.where(got_live, got_scores, -jnp.inf)
    new_scores = jnp.where(new_live, new_scores, -jnp.inf)
    top = jnp.maximum(
        jnp.maximum(jnp.max(old_scores, axis=2), jnp.max(got_scores, axis=2)),
        jnp.max(new_scores, axis=2),
    )[:, :, None]
    old_weights = jnp.exp(old_scores - top)
    got_weights = jnp.exp(got_scores - top)
    new_weights = jnp.exp(new_scores - top)
    total = (
        jnp.sum(old_weights, axis=2) + jnp.sum(got_weights, axis=2) + jnp.sum(new_weights, axis=2)
    )
    summed = jnp.einsum(
        "mpl,mlf->mpf",
        old_weights.astype(jnp.bfloat16),
        old_cache[:, :, :LAT],
        preferred_element_type=jnp.float32,
    )
    summed = summed + jnp.einsum(
        "sqk,kv->sqv",
        got_weights.astype(jnp.bfloat16),
        got_rows[:, :LAT],
        preferred_element_type=jnp.float32,
    )
    summed = summed + jnp.einsum(
        "mpl,mlf->mpf",
        new_weights.astype(jnp.bfloat16),
        new_latent[:, :, :LAT],
        preferred_element_type=jnp.float32,
    )
    return (summed / total[:, :, None]).astype(jnp.bfloat16).reshape(seq_dev, steps, heads_dev, LAT)


def experts(dec_states, moe_gain, expert_ids, route_weight, w_gate, w_up, w_down, prompts, attend):
    seq_dev, steps, d_part = dec_states.shape
    tok = seq_dev * steps
    topk = expert_ids.shape[-1]
    chips = lax.axis_size("ep") // 2
    core = lax.axis_index("ep") % 2
    y = 2 * lax.axis_index("tp") + lax.axis_index("section")

    def part_of(k):
        return group_of_y((y + k) % NY)

    wide = dec_states.reshape(tok, d_part).astype(jnp.float32)
    scaled = (wide * moe_gain).astype(jnp.bfloat16)
    meta = jnp.concatenate(
        [
            expert_ids.reshape(tok, topk).astype(jnp.float32),
            route_weight.reshape(tok, topk).astype(jnp.float32),
            jnp.sum(wide * wide, axis=1, keepdims=True),
        ],
        axis=1,
    )
    meta = jnp.concatenate([meta, other_core(meta)], axis=0)
    scaled = jnp.concatenate([scaled, other_core(scaled)], axis=0)
    downs = [
        over_y(lax.dynamic_slice_in_dim(w_down[0], part_of(k) * d_part, d_part, axis=1), k)
        for k in ORDER
    ]
    ids = meta[:, :topk].astype(jnp.int32)
    here = 2 * jnp.arange(chips, dtype=jnp.int32) + core
    named = ids.T[:, None, :] == here[None, :, None]
    chosen = slots(jnp.any(named, axis=0), tok, E_CAP)
    half = E_CAP // CHUNKS
    n = chips * 2 * half
    chosen = [chosen[:, :, c * half : (c + 1) * half] for c in range(CHUNKS)]
    pick = jnp.stack(chosen, axis=1).astype(jnp.bfloat16).reshape(CHUNKS * n, 2 * tok)

    def exchange(v):
        return chips_exchange(v.reshape(chips, v.shape[0] // chips, -1))

    rows = exchange(dot(pick, scaled).astype(jnp.bfloat16))
    squares = meta[:, 2 * topk]
    square_sum = squares
    for k in range(1, NY):
        square_sum = square_sum + over_y(squares, k)
    scale = lax.rsqrt(square_sum / (d_part * NY) + EPS)
    pieces, rest = [], scale
    for _ in range(3):
        pieces.append(lax.reduce_precision(rest, 8, 7))
        rest = rest - pieces[-1]
    pieces = jnp.stack(pieces, axis=1).astype(jnp.bfloat16)
    scales = jnp.concatenate(
        [dot(v.astype(jnp.bfloat16).reshape(n, 2 * tok), pieces) for v in chosen], axis=1
    ).astype(jnp.bfloat16)
    follow = jnp.concatenate([prompts[:, : -scales.shape[1]], scales], axis=1)
    rows, downs, follow, gate_w, up_w = lax.optimization_barrier(
        (rows, downs, follow, w_gate[0], w_up[0])
    )
    got = exchange(follow).reshape(n, -1)
    attn_out = attend(got)
    factors = [
        jnp.sum(got[:, at : at + 3].astype(jnp.float32), axis=1, keepdims=True)
        for at in (got.shape[1] - 6, got.shape[1] - 3)
    ]
    blocks = [
        lax.dynamic_slice_in_dim(source, part_of(k) * d_part, d_part, axis=0)
        for k in (0, NY - 1, 1, 2)
        for source in (gate_w, up_w)
    ]
    arrived = [
        rows[:, c * 2 * half : (c + 1) * 2 * half].reshape(n, d_part) for c in range(CHUNKS)
    ]

    def neighbours(rows):
        return over_y(rows, 1), over_y(rows, -1)

    def across(below, above):
        mid = n // 2
        return over_y(below[:mid], 1), over_y(above[mid:], -1)

    near = [neighbours(arrived[0])]
    near[0], arrived[1], blocks = lax.optimization_barrier((near[0], arrived[1], blocks))
    near.append(neighbours(arrived[1]))

    weight = meta[:, topk : 2 * topk]
    share = weight / jnp.sum(weight, axis=1, keepdims=True)
    gives = jnp.sum(jnp.where(named, share.T[:, None, :], 0.0), axis=0)
    mixes = []
    for v in chosen:
        mix = jnp.where(v, gives[:, None, None, :], 0.0).reshape(n, 2 * tok)
        high = lax.reduce_precision(mix, 8, 7)
        mixes.append([high.astype(jnp.bfloat16), (mix - high).astype(jnp.bfloat16)])
    mixed = 0.0
    contract = (((0,), (0,)), ((), ()))
    for c in range(CHUNKS):
        below, above = near[c]
        low, high = across(below, above)
        sums = near_sums(arrived[c], below, above, blocks[:6])
        hidden = hidden_units(low, high, sums, factors[c], *blocks[6:])
        hidden = [over_y(hidden, k) for k in ORDER]
        out = down_product(hidden, downs)
        if c == 0:
            out, near[1] = lax.optimization_barrier((out, near[1]))
        back = exchange(out).reshape(n, -1)
        if c == 1:
            back, attn_out, mixed, mixes = lax.optimization_barrier((back, attn_out, mixed, mixes))
        for part in mixes[c]:
            mixed = mixed + lax.dot_general(
                part, back, contract, preferred_element_type=jnp.float32
            )
    mixed = mixed[:tok] + other_core(mixed[tok:].astype(jnp.bfloat16)).astype(jnp.float32)
    return mixed.astype(jnp.bfloat16).reshape(seq_dev, steps, d_part), attn_out


def body(
    prompt_latent,
    prompt_dest,
    prompt_slot,
    old_cache,
    cache_len,
    new_latent,
    dec_query,
    dec_states,
    moe_gain,
    expert_ids,
    route_weight,
    w_gate,
    w_up,
    w_down,
):
    ep_index, n_ep = lax.axis_index("ep"), lax.axis_size("ep")
    prompts = prompt_rows(prompt_latent, prompt_dest, prompt_slot, n_ep // 2, ep_index % 2)

    def attend(got):
        return attention(got, old_cache, cache_len, new_latent, dec_query)

    moe_out, attn_out = experts(
        dec_states, moe_gain, expert_ids, route_weight, w_gate, w_up, w_down, prompts, attend
    )
    return (attn_out, moe_out)


def solution(mesh):
    placed = (
        P("ep", None),
        P("ep", None),
        P("ep"),
        P("ep", None, None),
        P("ep"),
        P("ep", None, None),
        P("ep", None, GROUP, None),
        P("ep", None, GROUP),
        P(GROUP),
        P("ep", None, None),
        P("ep", None, None),
        P("ep", None, GROUP),
        P("ep", None, GROUP),
        P("ep", GROUP, None),
    )
    return jax.shard_map(
        body,
        mesh=mesh,
        in_specs=placed,
        out_specs=(P("ep", None, GROUP, None), P("ep", None, GROUP)),
        check_vma=False,
    )
```
